32 devices in a mesh: groups: 2 (over y), blk: 4 (over z), cap: 2 (over x), yr: 2 (over core).
Axes of the slice: x: 2, y: 2, z: 4, core: 2. Of those that a mesh axis runs over, the one named last changes fastest.
Arguments:
- price: bfloat16 [16, 8, 64, 168], P(('groups', 'yr'), 'blk'), parts along dimension 0, may hold values from -0.5 to 0.5
- avail: bfloat16 [16, 8, 32, 168, 128], P(('groups', 'yr'), 'blk', 'cap'), parts along dimension 0, may hold values from 0 to 1
- tile_ids: int32 [16, 8, 32], P(('groups', 'yr'), 'blk', 'cap'), parts along dimension 0, may hold values from 0 to 255, as said below
- soc: bfloat16 [16, 8, 64, 4096], P(('groups', 'yr'), 'blk', None, 'cap'), parts along dimension 0, may hold values from -3 to 3
- link: bfloat16 [16, 8, 64, 4096], P(('groups', 'yr'), 'blk', None, 'cap'), parts along dimension 0, may hold values from -3 to 3
- retain: float32 [4096], P('cap'), may hold values from 0.3 to 1
- store_col: int32 [4096], P('cap'), may hold values from 0 to 32767, as said below
- weight: float32 [16, 8], P(('groups', 'yr'), 'blk'), parts along dimension 0, may hold values from 0.1 to 1
- capacity: float32 [65536], P('cap'), may hold values from 0.002 to 0.02
- objective: float32 [16, 8, 64], P(('groups', 'yr'), 'blk'), parts along dimension 0, may hold values from -6 to 6
Outputs:
- expected_cut: float32 [128, 2, 32768], P('groups', 'cap', ('blk', 'yr')), parts along dimension 0
- intercept: float32 [16, 8, 64], P(('groups', 'yr'), 'blk'), parts along dimension 0
The draws below stay inside these ranges and needn't reach their ends.
There are 2 independent parts, one for each index of `groups`. The reference program is written for one: setup_inputs(seed, part) draws one part's arguments, and reference() takes and returns one part's arrays. A program takes and returns all parts, laid end to end along the dimension named above; an argument that names none is the same for every part. Nothing has to cross between parts.
Inputs may be any that keep to these rules, and one draw needn't show every extreme that they name: `tile_ids`: within one week and one capacity shard (entries k with equal k // 16) the tile indices are distinct. `store_col`: within one shard of 2048 storage units the columns are distinct.
All inputs are finite; a program needn't handle non-finite values.
Results may differ from the reference program's by a relative error of at most 0.0003.
Values may be sent and summed in bfloat16 or wider, within the bound.
A program may use at most 128 MiB of HBM per device.

```python
import math
import jax
import jax.numpy as jnp
from jax import lax

C = 65536
S = 4096
H = 168
TW = 128
R = 64
K_DEV = 16
WEEKS = 8
YEARS = 8
K = 32
CAPS = 2
CDEV = 32768
S_DEV = 2048
TILES_DEV = 256


def draw_tile_ids(key, part):
    key = jax.random.fold_in(key, 11)
    count = YEARS * WEEKS * (K // K_DEV)
    keys = jax.random.split(key, count)
    picks = jax.vmap(lambda one: jax.random.permutation(one, TILES_DEV)[:K_DEV])(keys)
    return picks.reshape(YEARS, WEEKS, K).astype(jnp.int32)


def draw_store_col(key, part):
    key = jax.random.fold_in(key, 23)
    keys = jax.random.split(key, S // S_DEV)

    def one_shard(one):
        first_key, second_key = jax.random.split(one)
        inner = jax.random.permutation(first_key, CDEV - 2)[:S_DEV - 2] + 1
        full = jnp.concatenate([jnp.zeros((1,), jnp.int32), jnp.full((1,), CDEV - 1, jnp.int32), inner.astype(jnp.int32)])
        return jax.random.permutation(second_key, full)
    return jax.vmap(one_shard)(keys).reshape(S).astype(jnp.int32)


def shard_levels(stream_key, extent, pieces, least, largest):
    gain, own = 1.0, jax.random.fold_in(stream_key, 6)
    for position, shards_of in pieces:
        steps = jnp.exp(jax.random.uniform(jax.random.fold_in(own, position), (shards_of,), jnp.float32, least / len(pieces), largest / len(pieces)))
        gain = gain * jnp.repeat(steps, extent[position] // shards_of).reshape([-1 if axis == position else 1 for axis in range(len(extent))])
    return gain


def centred(own_key, extent, width, bound, cuts=(), dtype=jnp.bfloat16):
    factor_of = shard_levels(own_key, extent, cuts, -0.22, 0.18) if cuts else 1.0
    result = jax.random.normal(own_key, extent, jnp.float32) * width * factor_of
    return jnp.minimum(jnp.maximum(result, -bound), bound).astype(dtype)


def setup_inputs(seed: int = 0, part: int = 0) -> dict:
    arg_keys = jax.random.split(jax.random.key(seed), 11)
    part_keys = jax.random.split(jax.random.fold_in(arg_keys[10], part), 11)
    price = centred(part_keys[0], (YEARS, WEEKS, R, H), H ** -0.5, 0.5, ((0, 2), (1, 4)))
    avail = jnp.clip(1.0 * jax.random.uniform(part_keys[1], (YEARS, WEEKS, K, H, TW), jnp.float32) ** shard_levels(part_keys[1], (YEARS, WEEKS, K, H, TW), ((0, 2), (1, 4), (2, 2)), -0.2, 0.2), 0.0, 1.0).astype(jnp.bfloat16)
    tile_ids = draw_tile_ids(jax.random.fold_in(jax.random.fold_in(arg_keys[10], part), 71), part)
    soc = centred(part_keys[3], (YEARS, WEEKS, R, S), 0.5, 3.0, ((0, 2), (1, 4), (3, 2)))
    link = centred(part_keys[4], (YEARS, WEEKS, R, S), 0.5, 3.0, ((0, 2), (1, 4), (3, 2)))
    retain = jnp.clip(0.3 + 0.7 * jax.random.uniform(arg_keys[5], (S,), jnp.float32) ** shard_levels(arg_keys[5], (S,), ((0, 2),), -0.2, 0.2), 0.3, 1.0)
    store_col = draw_store_col(jax.random.fold_in(arg_keys[10], 71), part)
    weight = jnp.clip(jnp.exp(math.log(1.0) - 2.3025851 * jax.random.uniform(part_keys[7], (YEARS, WEEKS), jnp.float32) ** shard_levels(part_keys[7], (YEARS, WEEKS), ((0, 2), (1, 4)), -0.2, 0.2)), 0.1, 1.0)
    capacity = jnp.clip(jnp.exp(math.log(0.02) - 2.30258502 * jax.random.uniform(arg_keys[8], (C,), jnp.float32) ** shard_levels(arg_keys[8], (C,), ((0, 2),), -0.2, 0.2)), 0.002, 0.02)
    objective = centred(part_keys[9], (YEARS, WEEKS, R), 1.0, 6.0, ((0, 2), (1, 4)), jnp.float32)
    return {"price": price, "avail": avail, "tile_ids": tile_ids, "soc": soc, "link": link, "retain": retain, "store_col": store_col, "weight": weight, "capacity": capacity, "objective": objective}


def reference(price, avail, tile_ids, soc, link, retain, store_col, weight, capacity, objective):
    hi = lax.Precision.HIGHEST
    base = ((jnp.arange(K) // K_DEV) * (CDEV // TW)).astype(jnp.int32)
    store_glob = (store_col + (jnp.arange(S) // S_DEV) * CDEV).astype(jnp.int32)
    link_next = jnp.roll(link, -1, axis=1)
    stor = soc.astype(jnp.float32) + retain * link_next.astype(jnp.float32) - link.astype(jnp.float32)
    cap_tiles = capacity.reshape(C // TW, TW)
    cap_store = capacity[store_glob]

    def one_year(acc, items):
        price_y, avail_y, ids_y, stor_y, weight_y = items
        gcut = jnp.einsum('wrh,wkhc->wkrc', price_y.astype(jnp.float32), avail_y.astype(jnp.float32), precision=hi)
        glob = (ids_y + base[None, :]).astype(jnp.int32)
        contrib = gcut * weight_y[:, None, None, None]
        contrib = jnp.transpose(contrib, (2, 0, 1, 3)).reshape(R, WEEKS * K, TW)
        acc = acc.reshape(R, C // TW, TW).at[:, glob.reshape(-1)].add(contrib).reshape(R, C)
        xt = cap_tiles[glob]
        dots = jnp.sum(gcut * xt[:, :, None, :], axis=(1, 3))
        acc = acc.at[:, store_glob].add(jnp.sum(weight_y[:, None, None] * stor_y, axis=0))
        dots = dots + jnp.sum(stor_y * cap_store, axis=-1)
        return acc, dots

    acc0 = jnp.zeros((R, C), jnp.float32)
    acc, dots = lax.scan(one_year, acc0, (price, avail, tile_ids, stor, weight))
    return acc.reshape(R, CAPS, CDEV), objective - dots
```

```python
import functools

import jax
import jax.numpy as jnp
from jax import lax
from jax.experimental import pallas as pl
from jax.experimental.pallas import tpu as pltpu
from jax.sharding import PartitionSpec as P

MESH = pl.DeviceIdType.MESH
LANES = 128
VMEM_LIMIT = 48 * 1024 * 1024


def split3(value):
    hi = value.astype(jnp.bfloat16)
    rest = value - hi.astype(jnp.float32)
    mid = rest.astype(jnp.bfloat16)
    lo = (rest - mid.astype(jnp.float32)).astype(jnp.bfloat16)
    return hi, mid, lo


def local_kernel(
    years, weeks, ids_ref, weight_ref, price_ref, avail_ref, soc_ref, link_ref, retain_ref, col_ref, cap_ref,
    acc_ref, wsum_ref, d_ref, e_ref, caps_ref,
):
    step = pl.program_id(0)
    tiles = avail_ref.shape[2]
    rows = price_ref.shape[2]
    units = retain_ref.shape[1]
    tile_count = cap_ref.shape[0]

    @pl.when(step == 0)
    def _():
        def clear(i, carry):
            acc_ref[i] = jnp.zeros((rows, LANES), jnp.float32)
            return carry

        lax.fori_loop(0, tile_count, clear, 0)
        wsum_ref[...] = jnp.zeros_like(wsum_ref)
        d_ref[...] = jnp.zeros_like(d_ref)
        e_ref[...] = jnp.zeros_like(e_ref)
        turned = jnp.transpose(cap_ref[:, 0, :])
        parts = split3(turned)
        chunk = 512
        for first in range(0, units, chunk):
            col = col_ref[:, first:first + chunk]
            tile_of = lax.broadcasted_iota(jnp.int32, (tile_count, chunk), 0)
            pick = jnp.where(tile_of == (col >> 7), 1.0, 0.0).astype(jnp.bfloat16)
            found = jnp.zeros((LANES, chunk), jnp.float32)
            for part in parts:
                found += jnp.dot(part, pick, preferred_element_type=jnp.float32)
            lane_of = lax.broadcasted_iota(jnp.int32, (LANES, chunk), 0)
            found = jnp.where(lane_of == (col & 127), found, 0.0)
            caps_ref[:, first:first + chunk] = jnp.sum(found, axis=0, keepdims=True)

    here = weight_ref[step]
    inside = lax.rem(step, weeks)
    before = jnp.where(inside > 0, weight_ref[jnp.maximum(step - 1, 0)], 0.0)
    duals = price_ref[0, 0]
    tile_dots = jnp.zeros((rows, LANES), jnp.float32)
    for k in range(tiles):
        index = ids_ref[step * tiles + k]
        cut = jnp.dot(duals, avail_ref[0, 0, k], preferred_element_type=jnp.float32)
        tile_dots += cut * cap_ref[index]
        acc_ref[index] += here * cut

    lane = lax.broadcasted_iota(jnp.int32, (16, LANES), 1)
    last = (step // weeks) * weeks + weeks - 1
    d_ref[...] += jnp.where(
        lax.broadcasted_iota(jnp.int32, (rows, LANES), 1) == step, jnp.sum(tile_dots, axis=1, keepdims=True), 0.0
    )

    def band(i, carry):
        at = pl.ds(pl.multiple_of(i * 16, 16), 16)
        dots = jnp.zeros((16, LANES), jnp.float32)
        nexts = jnp.zeros((16, LANES), jnp.float32)
        for first in range(0, units, LANES):
            span = slice(first, first + LANES)
            s = soc_ref[0, 0, at, span].astype(jnp.float32)
            l = link_ref[0, 0, at, span].astype(jnp.float32)
            kept = retain_ref[:, span] * l
            flow = s - l
            worth = caps_ref[:, span]
            wsum_ref[at, span] += here * flow + before * kept
            dots += worth * flow
            nexts += worth * kept
        own = jnp.sum(dots, axis=1, keepdims=True)
        later = jnp.sum(nexts, axis=1, keepdims=True)
        d_ref[at, :] += jnp.where(lane == step, own, 0.0) + jnp.where((lane == step - 1) & (inside > 0), later, 0.0)
        e_ref[at, :] += jnp.where((lane == last) & (inside == 0), later, 0.0)
        return carry

    lax.fori_loop(0, rows // 16, band, 0)


def code(x):
    top = jnp.maximum(jnp.max(jnp.abs(x), axis=0, keepdims=True), 1e-30)
    q = jnp.round(x * (32767.0 / top)).astype(jnp.int32).astype(jnp.int16)
    return q, top * (1.0 / 32767.0)


def value_of(q, scale):
    return q.astype(jnp.int32).astype(jnp.float32) * scale


def reduce_kernel(
    nb, nc, acc_ref, wsum_ref, first_ref, retain_ref, tail_ref, d_ref, e_ref, col_ref, objective_ref,
    out_ref, intercept_ref,
    pair, q_out, s_out, q_in, s_in, tail_in, d_in, e_in, w_own, w_pair, wq_out, ws_out, wq_in, ws_in, w_tot, w_hl,
    onel, placed,
    pair_sem, q_sem, s_sem, tail_sem, d_sem, e_sem, wp_sem, wq_sem, ws_sem, wt_sem,
):
    b, c, u = lax.axis_index("blk"), lax.axis_index("cap"), lax.axis_index("yr")
    sib = 1 - u
    ahead, behind = lax.rem(b + 1, nb), lax.rem(b + nb - 1, nb)
    per = out_ref.shape[1] // LANES
    rows, units = wsum_ref.shape
    half = units // 2
    years = first_ref.shape[0]
    order = list(range(nb - 1, 0, -1))
    power = nb & (nb - 1) == 0

    def target(d):
        return b ^ d if power else lax.rem(b + d, nb)

    def source(d):
        return b ^ d if power else lax.rem(b + nb - d, nb)

    barrier = pltpu.get_barrier_semaphore()
    pl.semaphore_signal(barrier, inc=1, device_id={"yr": sib}, device_id_type=MESH)
    for d in order:
        pl.semaphore_signal(barrier, inc=1, device_id={"blk": source(d)}, device_id_type=MESH)
    for dc in range(1, nc):
        other = lax.rem(c + dc, nc)
        pl.semaphore_signal(barrier, inc=1, device_id={"cap": other}, device_id_type=MESH)
        pl.semaphore_signal(barrier, inc=1, device_id={"blk": ahead, "cap": other}, device_id_type=MESH)
    pl.semaphore_wait(barrier, 1 + (nb - 1) + 2 * (nc - 1))

    def remote(src, dst, sem, device):
        return pltpu.make_async_remote_copy(
            src_ref=src, dst_ref=dst, send_sem=sem.at[0], recv_sem=sem.at[1], device_id=device, device_id_type=MESH
        )

    tail_copy = remote(tail_ref, tail_in, tail_sem, {"blk": ahead})
    tail_copy.start()
    pair_copies = []
    for j, d in enumerate(order + [0]):
        start = pl.multiple_of((2 * target(d) + sib) * per, per)
        pair_copies.append(remote(acc_ref.at[pl.ds(start, per)], pair.at[j], pair_sem.at[j], {"yr": sib}))
    pair_copies[0].start()
    small = []
    for dc in range(1, nc):
        other = lax.rem(c + dc, nc)
        small.append(remote(d_ref, d_in.at[dc - 1], d_sem.at[dc - 1], {"cap": other}))
    for dc in range(nc):
        other = lax.rem(c + dc, nc)
        small.append(remote(e_ref, e_in.at[dc], e_sem.at[dc], {"blk": behind, "cap": other}))
    for copy in small:
        copy.start()

    tail_copy.wait()
    for h in range(2):
        for first in range(0, half, LANES):
            span = slice(h * half + first, h * half + first + LANES)

            def band(i, carry, h=h, first=first, span=span):
                at = pl.ds(pl.multiple_of(i * 16, 16), 16)
                total = jnp.zeros((16, LANES), jnp.float32)
                for y in range(years):
                    total += tail_in[y] * first_ref[y, 0, at, span].astype(jnp.float32)
                w_own[h, at, first:first + LANES] = wsum_ref[at, span] + retain_ref[:, span] * total
                return carry

            lax.fori_loop(0, rows // 16, band, 0)
    w_copy = remote(w_own.at[sib], w_pair, wp_sem, {"yr": sib})
    w_copy.start()
    for copy in pair_copies[1:]:
        copy.start()

    def send_piece(j):
        d = order[j]
        base = (2 * target(d) + u) * per

        def one(i, carry):
            q, s = code(acc_ref[base + i] + pair[j, i])
            q_out[j, i] = q
            s_out[j, pl.ds(i, 1)] = s
            return carry

        pair_copies[j].wait()
        lax.fori_loop(0, per, one, 0)
        copies = [
            remote(q_out.at[j], q_in.at[j], q_sem.at[j], {"blk": target(d)}),
            remote(s_out.at[j], s_in.at[j], s_sem.at[j], {"blk": target(d)}),
        ]
        for copy in copies:
            copy.start()
        return copies

    w_copy.wait()
    for first in range(0, half, LANES):
        span = slice(first, first + LANES)
        total = w_own[u, :, span] + w_pair[:, span]
        q, s = code(total)
        w_tot[u, :, span] = total
        wq_out[:, span] = q
        ws_out[:, span] = s
    w_copies = []
    for j, d in enumerate(order):
        w_copies.append(remote(wq_out, wq_in.at[j], wq_sem.at[j], {"blk": target(d)}))
        w_copies.append(remote(ws_out, ws_in.at[j], ws_sem.at[j], {"blk": target(d)}))
    for copy in w_copies:
        copy.start()

    sent = []
    for j in range(len(order)):
        sent.append(send_piece(j))

    for copy in w_copies:
        copy.wait()
    for first in range(0, half, LANES):
        span = slice(first, first + LANES)
        total = w_tot[u, :, span]
        for j in range(len(order)):
            total += value_of(wq_in[j, :, span], ws_in[j, :, span])
        w_tot[u, :, span] = total
    t_copy = remote(w_tot.at[u], w_tot.at[u], wt_sem, {"yr": sib})
    t_copy.start()
    chunk = 256
    for first in range(0, units, chunk):
        lane_of = lax.broadcasted_iota(jnp.int32, (LANES, chunk), 0)
        hot = jnp.where(lane_of == (col_ref[:, first:first + chunk] & 127), 1.0, 0.0)
        onel[first:first + chunk, :] = jnp.transpose(hot).astype(jnp.bfloat16)
    t_copy.wait()
    for h in range(2):
        total = w_tot[h]
        hi = total.astype(jnp.bfloat16)
        w_hl[:rows, h * half:(h + 1) * half] = hi
        w_hl[rows:, h * half:(h + 1) * half] = (total - hi.astype(jnp.float32)).astype(jnp.bfloat16)
    mine = (2 * b + u) * per

    def place(i, carry):
        mask = jnp.where((col_ref[...] >> 7) == mine + i, 1.0, 0.0).astype(jnp.bfloat16)
        both = jnp.dot(w_hl[...] * mask, onel[...], preferred_element_type=jnp.float32)
        placed[i] = both[:rows] + both[rows:]
        return carry

    lax.fori_loop(0, per, place, 0)

    pair_copies[-1].wait()
    for copies in sent:
        for copy in copies:
            copy.wait()

    def finish(i, carry):
        total = acc_ref[mine + i] + pair[nb - 1, i] + placed[i]
        for j in range(len(order)):
            total += value_of(q_in[j, i], s_in[j, pl.ds(i, 1)])
        out_ref[:, pl.ds(pl.multiple_of(i * LANES, LANES), LANES)] = total
        return carry

    lax.fori_loop(0, per, finish, 0)

    for copy in small:
        copy.wait()
    dots = d_ref[...]
    for dc in range(1, nc):
        dots += d_in[dc - 1]
    for dc in range(nc):
        dots += e_in[dc]
    intercept_ref[...] = objective_ref[...] - jnp.transpose(dots)[:objective_ref.shape[0], :]


def local(nb, nc, price, avail, tile_ids, soc, link, retain, store_col, weight, capacity, objective):
    years, weeks, tiles, hours, width = avail.shape
    rows, units = soc.shape[2:]
    columns = capacity.shape[0]
    tile_count = columns // width
    steps = years * weeks
    piece = columns // (2 * nb)
    per = piece // width
    half = units // 2
    retain2 = retain.reshape(1, units)
    col2 = store_col.reshape(1, units)
    f32 = jnp.float32

    def week(g, *_):
        return (g // weeks, lax.rem(g, weeks), 0, 0)

    def fixed(rank):
        return lambda g, *_: (0,) * rank

    acc, wsum, d, e = pl.pallas_call(
        functools.partial(local_kernel, years, weeks),
        grid_spec=pltpu.PrefetchScalarGridSpec(
            num_scalar_prefetch=2,
            grid=(steps,),
            in_specs=[
                pl.BlockSpec((1, 1, rows, hours), week),
                pl.BlockSpec((1, 1, tiles, hours, width), lambda g, *_: (g // weeks, lax.rem(g, weeks), 0, 0, 0)),
                pl.BlockSpec((1, 1, rows, units), week),
                pl.BlockSpec((1, 1, rows, units), week),
                pl.BlockSpec((1, units), fixed(2)),
                pl.BlockSpec((1, units), fixed(2)),
                pl.BlockSpec((tile_count, 1, width), fixed(3)),
            ],
            out_specs=[
                pl.BlockSpec((tile_count, rows, width), fixed(3)),
                pl.BlockSpec((rows, units), fixed(2)),
                pl.BlockSpec((rows, LANES), fixed(2)),
                pl.BlockSpec((rows, LANES), fixed(2)),
            ],
            scratch_shapes=[pltpu.VMEM((1, units), f32)],
        ),
        out_shape=[
            jax.ShapeDtypeStruct((tile_count, rows, width), f32),
            jax.ShapeDtypeStruct((rows, units), f32),
            jax.ShapeDtypeStruct((rows, LANES), f32),
            jax.ShapeDtypeStruct((rows, LANES), f32),
        ],
        compiler_params=pltpu.CompilerParams(vmem_limit_bytes=VMEM_LIMIT),
    )(tile_ids.reshape(-1), weight.reshape(-1), price, avail, soc, link, retain2, col2, capacity.reshape(tile_count, 1, width))

    tail = jnp.broadcast_to(weight[:, weeks - 1][:, None, None], (years, 1, LANES))
    vmem = pl.BlockSpec(memory_space=pltpu.VMEM)
    dma = pltpu.SemaphoreType.DMA
    out, intercept = pl.pallas_call(
        functools.partial(reduce_kernel, nb, nc),
        grid=(1,),
        in_specs=[vmem, vmem, pl.BlockSpec((years, 1, rows, units), lambda g: (0, 0, 0, 0))] + [vmem] * 6,
        out_specs=[vmem, vmem],
        out_shape=[
            jax.ShapeDtypeStruct((rows, piece), f32),
            jax.ShapeDtypeStruct((steps, rows), f32),
        ],
        scratch_shapes=[
            pltpu.VMEM((nb, per, rows, width), f32),
            pltpu.VMEM((nb - 1, per, rows, width), jnp.int16),
            pltpu.VMEM((nb - 1, per, width), f32),
            pltpu.VMEM((nb - 1, per, rows, width), jnp.int16),
            pltpu.VMEM((nb - 1, per, width), f32),
            pltpu.VMEM((years, 1, LANES), f32),
            pltpu.VMEM((max(nc - 1, 1), rows, LANES), f32),
            pltpu.VMEM((nc, rows, LANES), f32),
            pltpu.VMEM((2, rows, half), f32),
            pltpu.VMEM((rows, half), f32),
            pltpu.VMEM((rows, half), jnp.int16),
            pltpu.VMEM((1, half), f32),
            pltpu.VMEM((nb - 1, rows, half), jnp.int16),
            pltpu.VMEM((nb - 1, 1, half), f32),
            pltpu.VMEM((2, rows, half), f32),
            pltpu.VMEM((2 * rows, units), jnp.bfloat16),
            pltpu.VMEM((units, LANES), jnp.bfloat16),
            pltpu.VMEM((per, rows, width), f32),
            dma((nb, 2)),
            dma((nb - 1, 2)),
            dma((nb - 1, 2)),
            dma((2,)),
            dma((max(nc - 1, 1), 2)),
            dma((nc, 2)),
            dma((2,)),
            dma((nb - 1, 2)),
            dma((nb - 1, 2)),
            dma((2,)),
        ],
        compiler_params=pltpu.CompilerParams(
            collective_id=0, has_side_effects=True, vmem_limit_bytes=VMEM_LIMIT
        ),
    )(acc, wsum, link, retain2, tail, d, e, col2, objective.reshape(steps, rows))
    return (out[:, None, :], intercept.reshape(years, weeks, rows))


def solution(mesh):
    return jax.shard_map(
        functools.partial(local, mesh.shape["blk"], mesh.shape["cap"]),
        mesh=mesh,
        in_specs=(
            P(("groups", "yr"), "blk", None, None),
            P(("groups", "yr"), "blk", "cap", None, None),
            P(("groups", "yr"), "blk", "cap"),
            P(("groups", "yr"), "blk", None, "cap"),
            P(("groups", "yr"), "blk", None, "cap"),
            P("cap"),
            P("cap"),
            P(("groups", "yr"), "blk"),
            P("cap"),
            P(("groups", "yr"), "blk", None),
        ),
        out_specs=(P("groups", "cap", ("blk", "yr")), P(("groups", "yr"), "blk", None)),
        check_vma=False,
    )
```

```python
import functools

import jax
import jax.numpy as jnp
from jax import lax
from jax.experimental import pallas as pl
from jax.experimental.pallas import tpu as pltpu
from jax.sharding import PartitionSpec as P

MESH = pl.DeviceIdType.MESH
LANES = 128
VMEM_LIMIT = 60 * 1024 * 1024


def split3(value):
    hi = value.astype(jnp.bfloat16)
    rest = value - hi.astype(jnp.float32)
    mid = rest.astype(jnp.bfloat16)
    lo = (rest - mid.astype(jnp.float32)).astype(jnp.bfloat16)
    return hi, mid, lo


def local_kernel(
    years, weeks, ids_ref, weight_ref, price_ref, avail_ref, soc_ref, link_ref, retain_ref, col_ref, cap_ref,
    acc_ref, wsum_ref, d_ref, e_ref, caps_ref,
):
    step = pl.program_id(0)
    tiles = avail_ref.shape[2]
    rows = price_ref.shape[2]
    units = retain_ref.shape[1]
    tile_count = cap_ref.shape[0]

    @pl.when(step == 0)
    def _():
        def clear(i, carry):
            acc_ref[i] = jnp.zeros((rows, LANES), jnp.float32)
            return carry

        lax.fori_loop(0, tile_count, clear, 0)
        wsum_ref[...] = jnp.zeros_like(wsum_ref)
        d_ref[...] = jnp.zeros_like(d_ref)
        e_ref[...] = jnp.zeros_like(e_ref)
        turned = jnp.transpose(cap_ref[:, 0, :])
        parts = split3(turned)
        chunk = 512
        for first in range(0, units, chunk):
            col = col_ref[:, first:first + chunk]
            tile_of = lax.broadcasted_iota(jnp.int32, (tile_count, chunk), 0)
            pick = jnp.where(tile_of == (col >> 7), 1.0, 0.0).astype(jnp.bfloat16)
            found = jnp.zeros((LANES, chunk), jnp.float32)
            for part in parts:
                found += jnp.dot(part, pick, preferred_element_type=jnp.float32)
            lane_of = lax.broadcasted_iota(jnp.int32, (LANES, chunk), 0)
            found = jnp.where(lane_of == (col & 127), found, 0.0)
            caps_ref[:, first:first + chunk] = jnp.sum(found, axis=0, keepdims=True)

    here = weight_ref[step]
    inside = lax.rem(step, weeks)
    before = jnp.where(inside > 0, weight_ref[jnp.maximum(step - 1, 0)], 0.0)
    duals = price_ref[0, 0]
    tile_dots = jnp.zeros((rows, LANES), jnp.float32)
    for k in range(tiles):
        index = ids_ref[step * tiles + k]
        cut = jnp.dot(duals, avail_ref[0, 0, k], preferred_element_type=jnp.float32)
        tile_dots += cut * cap_ref[index]
        acc_ref[index] += here * cut

    lane = lax.broadcasted_iota(jnp.int32, (16, LANES), 1)
    last = (step // weeks) * weeks + weeks - 1
    d_ref[...] += jnp.where(
        lax.broadcasted_iota(jnp.int32, (rows, LANES), 1) == step, jnp.sum(tile_dots, axis=1, keepdims=True), 0.0
    )

    def band(i, carry):
        at = pl.ds(pl.multiple_of(i * 16, 16), 16)
        dots = jnp.zeros((16, LANES), jnp.float32)
        nexts = jnp.zeros((16, LANES), jnp.float32)
        for first in range(0, units, LANES):
            span = slice(first, first + LANES)
            s = soc_ref[0, 0, at, span].astype(jnp.float32)
            l = link_ref[0, 0, at, span].astype(jnp.float32)
            kept = retain_ref[:, span] * l
            flow = s - l
            worth = caps_ref[:, span]
            wsum_ref[at, span] += here * flow + before * kept
            dots += worth * flow
            nexts += worth * kept
        own = jnp.sum(dots, axis=1, keepdims=True)
        later = jnp.sum(nexts, axis=1, keepdims=True)
        d_ref[at, :] += jnp.where(lane == step, own, 0.0) + jnp.where((lane == step - 1) & (inside > 0), later, 0.0)
        e_ref[at, :] += jnp.where((lane == last) & (inside == 0), later, 0.0)
        return carry

    lax.fori_loop(0, rows // 16, band, 0)


def code(x):
    top = jnp.maximum(jnp.max(jnp.abs(x), axis=0, keepdims=True), 1e-30)
    q = jnp.round(x * (32767.0 / top)).astype(jnp.int32).astype(jnp.int16)
    return q, top * (1.0 / 32767.0)


def value_of(q, scale):
    return q.astype(jnp.int32).astype(jnp.float32) * scale


def reduce_kernel(
    nb, nc, subs, acc_ref, wsum_ref, first_ref, retain_ref, tail_ref, d_ref, e_ref, col_ref, objective_ref,
    out_ref, intercept_ref,
    mine, pair, q_out, s_out, q_in, s_in, tail_in, d_in, e_in, w_own, w_pair, wq_out, ws_out, wq_in, ws_in, w_tot,
    w_hl, onel, placed,
    mine_sem, pair_sem, q_sem, s_sem, tail_sem, d_sem, e_sem, wp_sem, wq_sem, ws_sem, wt_sem,
):
    b, c, u = lax.axis_index("blk"), lax.axis_index("cap"), lax.axis_index("yr")
    sib = 1 - u
    ahead, behind = lax.rem(b + 1, nb), lax.rem(b + nb - 1, nb)
    per = out_ref.shape[1] // LANES
    rows, units = wsum_ref.shape
    half = units // 2
    years = first_ref.shape[0]
    share = per // subs
    sequence = []
    for k in range(nb):
        for t in (nb - 1 - k, k):
            if t not in sequence:
                sequence.append(t)

    barrier = pltpu.get_barrier_semaphore()
    pl.semaphore_signal(barrier, inc=1, device_id={"yr": sib}, device_id_type=MESH)
    pl.semaphore_signal(barrier, inc=1, device_id={"blk": ahead}, device_id_type=MESH)
    pl.semaphore_signal(barrier, inc=1, device_id={"blk": behind}, device_id_type=MESH)
    for dc in range(1, nc):
        other = lax.rem(c + dc, nc)
        pl.semaphore_signal(barrier, inc=1, device_id={"cap": other}, device_id_type=MESH)
        pl.semaphore_signal(barrier, inc=1, device_id={"blk": ahead, "cap": other}, device_id_type=MESH)
    local_copies = {}
    for t in sequence:
        start = pl.multiple_of((2 * t + u) * per, per)
        local_copies[t] = pltpu.make_async_copy(acc_ref.at[pl.ds(start, per)], mine.at[t], mine_sem.at[t])
        local_copies[t].start()
    pl.semaphore_wait(barrier, 3 + 2 * (nc - 1))

    def remote(src, dst, sem, device):
        return pltpu.make_async_remote_copy(
            src_ref=src, dst_ref=dst, send_sem=sem.at[0], recv_sem=sem.at[1], device_id=device, device_id_type=MESH
        )

    tail_copy = remote(tail_ref, tail_in, tail_sem, {"blk": ahead})
    tail_copy.start()
    pair_copies = {}
    for t in sequence:
        start = pl.multiple_of((2 * t + sib) * per, per)
        pair_copies[t] = remote(acc_ref.at[pl.ds(start, per)], pair.at[t], pair_sem.at[t], {"yr": sib})
    pair_copies[sequence[0]].start()

    tail_copy.wait()
    for h in range(2):
        for first in range(0, half, LANES):
            span = slice(h * half + first, h * half + first + LANES)

            def band(i, carry, h=h, first=first, span=span):
                at = pl.ds(pl.multiple_of(i * 16, 16), 16)
                total = jnp.zeros((16, LANES), jnp.float32)
                for y in range(years):
                    total += tail_in[y] * first_ref[y, 0, at, span].astype(jnp.float32)
                w_own[h, at, first:first + LANES] = wsum_ref[at, span] + retain_ref[:, span] * total
                return carry

            lax.fori_loop(0, rows // 16, band, 0)
    w_copy = remote(w_own.at[sib], w_pair, wp_sem, {"yr": sib})
    w_copy.start()
    for t in sequence[1:]:
        pair_copies[t].start()
    small = []
    for dc in range(1, nc):
        other = lax.rem(c + dc, nc)
        small.append(remote(d_ref, d_in.at[dc - 1], d_sem.at[dc - 1], {"cap": other}))
    for dc in range(nc):
        other = lax.rem(c + dc, nc)
        small.append(remote(e_ref, e_in.at[dc], e_sem.at[dc], {"blk": behind, "cap": other}))
    for copy in small:
        copy.start()

    toward = (ahead, behind)
    starts = (b == 0, b == nb - 1)
    ends = (b == nb - 1, b == 0)

    def store_copies(way):
        return (
            remote(wq_out.at[way], wq_in.at[way], wq_sem.at[way], {"blk": toward[way]}),
            remote(ws_out.at[way], ws_in.at[way], ws_sem.at[way], {"blk": toward[way]}),
        )

    def store_send(way, add):
        copies = store_copies(way)
        if add:
            for copy in copies:
                copy.wait_recv()
        for first in range(0, half, LANES):
            span = slice(first, first + LANES)
            total = w_tot[u, :, span]
            if add:
                total += value_of(wq_in[way, :, span], ws_in[way, :, span])
            q, s = code(total)
            wq_out[way, :, span] = q
            ws_out[way, :, span] = s
        for copy in copies:
            copy.start()

    w_copy.wait()
    for first in range(0, half, LANES):
        span = slice(first, first + LANES)
        w_tot[u, :, span] = w_own[u, :, span] + w_pair[:, span]
    for way in range(2):
        pl.when(starts[way])(functools.partial(store_send, way, False))
    for way in range(2):
        pl.when(jnp.logical_not(starts[way] | ends[way]))(functools.partial(store_send, way, True))

    def piece_copies(way, t, n):
        at = pl.ds(n * share, share)
        return (
            remote(q_out.at[t, at], q_in.at[way, t, at], q_sem.at[way, t, n], {"blk": toward[way]}),
            remote(s_out.at[t, n], s_in.at[way, t, n], s_sem.at[way, t, n], {"blk": toward[way]}),
        )

    def piece_send(way, t, n, add):
        copies = piece_copies(way, t, n)
        if add:
            for copy in copies:
                copy.wait_recv()

        def one(i, carry):
            at = n * share + i
            x = mine[t, at] + pair[t, at]
            if add:
                x += value_of(q_in[way, t, at], s_in[way, t, n, pl.ds(i, 1)])
            q, s = code(x)
            q_out[t, at] = q
            s_out[t, n, pl.ds(i, 1)] = s
            return carry

        lax.fori_loop(0, share, one, 0)
        for copy in copies:
            copy.start()

    def passes(way, t):
        return (b < t) if way == 0 else (b > t)

    def collect():
        for way in range(2):

            @pl.when(jnp.logical_not(starts[way]))
            def _(way=way):
                @pl.when(ends[way])
                def _():
                    for copy in store_copies(way):
                        copy.wait_recv()

                for first in range(0, half, LANES):
                    span = slice(first, first + LANES)
                    w_tot[u, :, span] += value_of(wq_in[way, :, span], ws_in[way, :, span])

        t_copy = remote(w_tot.at[u], w_tot.at[u], wt_sem, {"yr": sib})
        t_copy.start()
        chunk = 256
        for first in range(0, units, chunk):
            lane_of = lax.broadcasted_iota(jnp.int32, (LANES, chunk), 0)
            hot = jnp.where(lane_of == (col_ref[:, first:first + chunk] & 127), 1.0, 0.0)
            onel[first:first + chunk, :] = jnp.transpose(hot).astype(jnp.bfloat16)
        t_copy.wait()
        for h in range(2):
            total = w_tot[h]
            hi = total.astype(jnp.bfloat16)
            w_hl[:rows, h * half:(h + 1) * half] = hi
            w_hl[rows:, h * half:(h + 1) * half] = (total - hi.astype(jnp.float32)).astype(jnp.bfloat16)

    base = (2 * b + u) * per

    def place(i, carry):
        mask = jnp.where((col_ref[...] >> 7) == base + i, 1.0, 0.0).astype(jnp.bfloat16)
        both = jnp.dot(w_hl[...] * mask, onel[...], preferred_element_type=jnp.float32)
        placed[i] = both[:rows] + both[rows:]
        return carry

    slots = max((nb - 2) * subs, 1)
    quota = -(-per // slots)
    done = 0
    waited = set()
    for k in range(nb - 1):
        for t in (nb - 1 - k, k):
            if t not in waited:
                waited.add(t)
                local_copies[t].wait()
                pair_copies[t].wait()
        for n in range(subs):
            for way, t in ((0, nb - 1 - k), (1, k)):
                sends = passes(way, t)
                pl.when(sends & starts[way])(functools.partial(piece_send, way, t, n, False))
                pl.when(sends & jnp.logical_not(starts[way]))(functools.partial(piece_send, way, t, n, True))
            if k > 0 and done < per:
                upto = min(per, done + quota)
                lax.fori_loop(done, upto, place, 0)
                done = upto
        if k == 0:
            collect()
    if done < per:
        lax.fori_loop(done, per, place, 0)
    for t in sequence:
        if t not in waited:
            local_copies[t].wait()
            pair_copies[t].wait()

    def finish(t, ways):
        for n in range(subs):
            for way in ways:
                for copy in piece_copies(way, t, n):
                    copy.wait_recv()

            def one(i, carry):
                at = n * share + i
                total = mine[t, at] + pair[t, at] + placed[at]
                for way in ways:
                    total += value_of(q_in[way, t, at], s_in[way, t, n, pl.ds(i, 1)])
                out_ref[:, pl.ds(pl.multiple_of(at * LANES, LANES), LANES)] = total
                return carry

            lax.fori_loop(0, share, one, 0)

    for t in range(nb):
        ways = ([0] if t > 0 else []) + ([1] if t < nb - 1 else [])
        pl.when(b == t)(functools.partial(finish, t, ways))

    for copy in small:
        copy.wait()
    dots = d_ref[...]
    for dc in range(1, nc):
        dots += d_in[dc - 1]
    for dc in range(nc):
        dots += e_in[dc]
    intercept_ref[...] = objective_ref[...] - jnp.transpose(dots)[:objective_ref.shape[0], :]

    def settle(copies):
        for copy in copies:
            copy.wait_send()

    for way in range(2):
        pl.when(jnp.logical_not(ends[way]))(lambda way=way: settle(store_copies(way)))
    for way in range(2):
        for t in range(nb):
            if (way == 0 and t > 0) or (way == 1 and t < nb - 1):
                for n in range(subs):
                    pl.when(passes(way, t))(lambda way=way, t=t, n=n: settle(piece_copies(way, t, n)))


def local(nb, nc, price, avail, tile_ids, soc, link, retain, store_col, weight, capacity, objective):
    years, weeks, tiles, hours, width = avail.shape
    rows, units = soc.shape[2:]
    columns = capacity.shape[0]
    tile_count = columns // width
    steps = years * weeks
    piece = columns // (2 * nb)
    per = piece // width
    half = units // 2
    retain2 = retain.reshape(1, units)
    col2 = store_col.reshape(1, units)
    f32 = jnp.float32

    def week(g, *_):
        return (g // weeks, lax.rem(g, weeks), 0, 0)

    def fixed(rank):
        return lambda g, *_: (0,) * rank

    acc, wsum, d, e = pl.pallas_call(
        functools.partial(local_kernel, years, weeks),
        grid_spec=pltpu.PrefetchScalarGridSpec(
            num_scalar_prefetch=2,
            grid=(steps,),
            in_specs=[
                pl.BlockSpec((1, 1, rows, hours), week),
                pl.BlockSpec((1, 1, tiles, hours, width), lambda g, *_: (g // weeks, lax.rem(g, weeks), 0, 0, 0)),
                pl.BlockSpec((1, 1, rows, units), week),
                pl.BlockSpec((1, 1, rows, units), week),
                pl.BlockSpec((1, units), fixed(2)),
                pl.BlockSpec((1, units), fixed(2)),
                pl.BlockSpec((tile_count, 1, width), fixed(3)),
            ],
            out_specs=[
                pl.BlockSpec((tile_count, rows, width), fixed(3)),
                pl.BlockSpec((rows, units), fixed(2)),
                pl.BlockSpec((rows, LANES), fixed(2)),
                pl.BlockSpec((rows, LANES), fixed(2)),
            ],
            scratch_shapes=[pltpu.VMEM((1, units), f32)],
        ),
        out_shape=[
            jax.ShapeDtypeStruct((tile_count, rows, width), f32),
            jax.ShapeDtypeStruct((rows, units), f32),
            jax.ShapeDtypeStruct((rows, LANES), f32),
            jax.ShapeDtypeStruct((rows, LANES), f32),
        ],
        compiler_params=pltpu.CompilerParams(vmem_limit_bytes=VMEM_LIMIT),
    )(tile_ids.reshape(-1), weight.reshape(-1), price, avail, soc, link, retain2, col2, capacity.reshape(tile_count, 1, width))

    tail = jnp.broadcast_to(weight[:, weeks - 1][:, None, None], (years, 1, LANES))
    vmem = pl.BlockSpec(memory_space=pltpu.VMEM)
    dma = pltpu.SemaphoreType.DMA
    subs = max(per // 8, 1)
    out, intercept = pl.pallas_call(
        functools.partial(reduce_kernel, nb, nc, subs),
        grid=(1,),
        in_specs=[pl.BlockSpec(memory_space=pl.ANY), vmem]
        + [pl.BlockSpec((years, 1, rows, units), lambda g: (0, 0, 0, 0))]
        + [vmem] * 6,
        out_specs=[vmem, vmem],
        out_shape=[
            jax.ShapeDtypeStruct((rows, piece), f32),
            jax.ShapeDtypeStruct((steps, rows), f32),
        ],
        scratch_shapes=[
            pltpu.VMEM((nb, per, rows, width), f32),
            pltpu.VMEM((nb, per, rows, width), f32),
            pltpu.VMEM((nb, per, rows, width), jnp.int16),
            pltpu.VMEM((nb, subs, per // subs, width), f32),
            pltpu.VMEM((2, nb, per, rows, width), jnp.int16),
            pltpu.VMEM((2, nb, subs, per // subs, width), f32),
            pltpu.VMEM((years, 1, LANES), f32),
            pltpu.VMEM((max(nc - 1, 1), rows, LANES), f32),
            pltpu.VMEM((nc, rows, LANES), f32),
            pltpu.VMEM((2, rows, half), f32),
            pltpu.VMEM((rows, half), f32),
            pltpu.VMEM((2, rows, half), jnp.int16),
            pltpu.VMEM((2, 1, half), f32),
            pltpu.VMEM((2, rows, half), jnp.int16),
            pltpu.VMEM((2, 1, half), f32),
            pltpu.VMEM((2, rows, half), f32),
            pltpu.VMEM((2 * rows, units), jnp.bfloat16),
            pltpu.VMEM((units, LANES), jnp.bfloat16),
            pltpu.VMEM((per, rows, width), f32),
            dma((nb,)),
            dma((nb, 2)),
            dma((2, nb, subs, 2)),
            dma((2, nb, subs, 2)),
            dma((2,)),
            dma((max(nc - 1, 1), 2)),
            dma((nc, 2)),
            dma((2,)),
            dma((2, 2)),
            dma((2, 2)),
            dma((2,)),
        ],
        compiler_params=pltpu.CompilerParams(
            collective_id=0, has_side_effects=True, vmem_limit_bytes=VMEM_LIMIT
        ),
    )(acc, wsum, link, retain2, tail, d, e, col2, objective.reshape(steps, rows))
    return (out[:, None, :], intercept.reshape(years, weeks, rows))


def solution(mesh):
    return jax.shard_map(
        functools.partial(local, mesh.shape["blk"], mesh.shape["cap"]),
        mesh=mesh,
        in_specs=(
            P(("groups", "yr"), "blk", None, None),
            P(("groups", "yr"), "blk", "cap", None, None),
            P(("groups", "yr"), "blk", "cap"),
            P(("groups", "yr"), "blk", None, "cap"),
            P(("groups", "yr"), "blk", None, "cap"),
            P("cap"),
            P("cap"),
            P(("groups", "yr"), "blk"),
            P("cap"),
            P(("groups", "yr"), "blk", None),
        ),
        out_specs=(P("groups", "cap", ("blk", "yr")), P(("groups", "yr"), "blk", None)),
        check_vma=False,
    )
```

```python
import functools

import jax
import jax.numpy as jnp
from jax import lax
from jax.experimental import pallas as pl
from jax.experimental.pallas import tpu as pltpu
from jax.sharding import PartitionSpec as P

MESH = pl.DeviceIdType.MESH
LANES = 128
VMEM_LIMIT = 48 * 1024 * 1024


def split3(value):
    hi = value.astype(jnp.bfloat16)
    rest = value - hi.astype(jnp.float32)
    mid = rest.astype(jnp.bfloat16)
    lo = (rest - mid.astype(jnp.float32)).astype(jnp.bfloat16)
    return hi, mid, lo


def local_kernel(
    years, weeks, ids_ref, weight_ref, price_ref, avail_ref, soc_ref, link_ref, retain_ref, col_ref, cap_ref,
    acc_ref, wsum_ref, d_ref, e_ref, caps_ref,
):
    step = pl.program_id(0)
    tiles = avail_ref.shape[2]
    rows = price_ref.shape[2]
    units = retain_ref.shape[1]
    tile_count = cap_ref.shape[0]

    @pl.when(step == 0)
    def _():
        def clear(i, carry):
            acc_ref[i] = jnp.zeros((rows, LANES), jnp.float32)
            return carry

        lax.fori_loop(0, tile_count, clear, 0)
        wsum_ref[...] = jnp.zeros_like(wsum_ref)
        d_ref[...] = jnp.zeros_like(d_ref)
        e_ref[...] = jnp.zeros_like(e_ref)
        turned = jnp.transpose(cap_ref[:, 0, :])
        parts = split3(turned)
        chunk = 512
        for first in range(0, units, chunk):
            col = col_ref[:, first:first + chunk]
            tile_of = lax.broadcasted_iota(jnp.int32, (tile_count, chunk), 0)
            pick = jnp.where(tile_of == (col >> 7), 1.0, 0.0).astype(jnp.bfloat16)
            found = jnp.zeros((LANES, chunk), jnp.float32)
            for part in parts:
                found += jnp.dot(part, pick, preferred_element_type=jnp.float32)
            lane_of = lax.broadcasted_iota(jnp.int32, (LANES, chunk), 0)
            found = jnp.where(lane_of == (col & 127), found, 0.0)
            caps_ref[:, first:first + chunk] = jnp.sum(found, axis=0, keepdims=True)

    year, inside = step // weeks, lax.rem(step, weeks)
    here = weight_ref[year, inside]
    before = jnp.where(inside > 0, weight_ref[year, jnp.maximum(inside - 1, 0)], 0.0)
    duals = price_ref[0, 0]
    tile_dots = jnp.zeros((rows, LANES), jnp.float32)
    for k in range(tiles):
        index = ids_ref[year, inside, k]
        cut = jnp.dot(duals, avail_ref[0, 0, k], preferred_element_type=jnp.float32)
        tile_dots += cut * cap_ref[index]
        acc_ref[index] += here * cut

    lane = lax.broadcasted_iota(jnp.int32, (16, LANES), 1)
    last = (step // weeks) * weeks + weeks - 1
    d_ref[...] += jnp.where(
        lax.broadcasted_iota(jnp.int32, (rows, LANES), 1) == step, jnp.sum(tile_dots, axis=1, keepdims=True), 0.0
    )

    def band(i, carry):
        at = pl.ds(pl.multiple_of(i * 16, 16), 16)
        dots = jnp.zeros((16, LANES), jnp.float32)
        nexts = jnp.zeros((16, LANES), jnp.float32)
        for first in range(0, units, LANES):
            span = slice(first, first + LANES)
            s = soc_ref[0, 0, at, span].astype(jnp.float32)
            l = link_ref[0, 0, at, span].astype(jnp.float32)
            kept = retain_ref[:, span] * l
            flow = s - l
            worth = caps_ref[:, span]
            wsum_ref[at, span] += here * flow + before * kept
            dots += worth * flow
            nexts += worth * kept
        own = jnp.sum(dots, axis=1, keepdims=True)
        later = jnp.sum(nexts, axis=1, keepdims=True)
        d_ref[at, :] += jnp.where(lane == step, own, 0.0) + jnp.where((lane == step - 1) & (inside > 0), later, 0.0)
        e_ref[at, :] += jnp.where((lane == last) & (inside == 0), later, 0.0)
        return carry

    lax.fori_loop(0, rows // 16, band, 0)


def code(x):
    top = jnp.maximum(jnp.max(jnp.abs(x), axis=0, keepdims=True), 1e-30)
    q = jnp.round(x * (32767.0 / top)).astype(jnp.int32).astype(jnp.int16)
    return q, top * (1.0 / 32767.0)


def value_of(q, scale):
    return q.astype(jnp.int32).astype(jnp.float32) * scale


def reduce_kernel(
    nb, nc, acc_ref, wsum_ref, first_ref, retain_ref, tail_ref, d_ref, e_ref, col_ref, objective_ref,
    out_ref, intercept_ref,
    pair, q_out, s_out, q_in, s_in, tail_in, d_in, e_in, w_own, w_pair, wq_out, ws_out, wq_in, ws_in, w_tot, w_hl,
    onel, placed,
    pair_sem, q_sem, s_sem, tail_sem, d_sem, e_sem, wp_sem, wq_sem, ws_sem, wt_sem,
):
    b, c, u = lax.axis_index("blk"), lax.axis_index("cap"), lax.axis_index("yr")
    sib = 1 - u
    ahead, behind = lax.rem(b + 1, nb), lax.rem(b + nb - 1, nb)
    per = out_ref.shape[1] // LANES
    rows, units = wsum_ref.shape
    half = units // 2
    years = first_ref.shape[0]
    order = list(range(nb - 1, 0, -1))
    power = nb & (nb - 1) == 0

    def target(d):
        return b ^ d if power else lax.rem(b + d, nb)

    def source(d):
        return b ^ d if power else lax.rem(b + nb - d, nb)

    barrier = pltpu.get_barrier_semaphore()
    pl.semaphore_signal(barrier, inc=1, device_id={"yr": sib}, device_id_type=MESH)
    for d in order:
        pl.semaphore_signal(barrier, inc=1, device_id={"blk": source(d)}, device_id_type=MESH)
    for dc in range(1, nc):
        other = lax.rem(c + dc, nc)
        pl.semaphore_signal(barrier, inc=1, device_id={"cap": other}, device_id_type=MESH)
        pl.semaphore_signal(barrier, inc=1, device_id={"blk": ahead, "cap": other}, device_id_type=MESH)
    pl.semaphore_wait(barrier, 1 + (nb - 1) + 2 * (nc - 1))

    def remote(src, dst, sem, device):
        return pltpu.make_async_remote_copy(
            src_ref=src, dst_ref=dst, send_sem=sem.at[0], recv_sem=sem.at[1], device_id=device, device_id_type=MESH
        )

    tail_copy = remote(tail_ref, tail_in, tail_sem, {"blk": ahead})
    tail_copy.start()
    pair_copies = []
    for j, d in enumerate(order + [0]):
        start = pl.multiple_of((2 * target(d) + sib) * per, per)
        pair_copies.append(remote(acc_ref.at[pl.ds(start, per)], pair.at[j], pair_sem.at[j], {"yr": sib}))
    pair_copies[0].start()
    small = []
    for dc in range(1, nc):
        other = lax.rem(c + dc, nc)
        small.append(remote(d_ref, d_in.at[dc - 1], d_sem.at[dc - 1], {"cap": other}))
    for dc in range(nc):
        other = lax.rem(c + dc, nc)
        small.append(remote(e_ref, e_in.at[dc], e_sem.at[dc], {"blk": behind, "cap": other}))
    for copy in small:
        copy.start()

    tail_copy.wait()
    for h in range(2):
        for first in range(0, half, LANES):
            span = slice(h * half + first, h * half + first + LANES)

            def band(i, carry, h=h, first=first, span=span):
                at = pl.ds(pl.multiple_of(i * 16, 16), 16)
                total = jnp.zeros((16, LANES), jnp.float32)
                for y in range(years):
                    total += tail_in[y] * first_ref[y, 0, at, span].astype(jnp.float32)
                w_own[h, at, first:first + LANES] = wsum_ref[at, span] + retain_ref[:, span] * total
                return carry

            lax.fori_loop(0, rows // 16, band, 0)
    w_copy = remote(w_own.at[sib], w_pair, wp_sem, {"yr": sib})
    w_copy.start()
    for copy in pair_copies[1:]:
        copy.start()

    def send_piece(j):
        d = order[j]
        base = (2 * target(d) + u) * per

        def one(i, carry):
            q, s = code(acc_ref[base + i] + pair[j, i])
            q_out[j, i] = q
            s_out[j, pl.ds(i, 1)] = s
            return carry

        pair_copies[j].wait()
        lax.fori_loop(0, per, one, 0)
        copies = [
            remote(q_out.at[j], q_in.at[j], q_sem.at[j], {"blk": target(d)}),
            remote(s_out.at[j], s_in.at[j], s_sem.at[j], {"blk": target(d)}),
        ]
        for copy in copies:
            copy.start()
        return copies

    w_copy.wait()
    for first in range(0, half, LANES):
        span = slice(first, first + LANES)
        total = w_own[u, :, span] + w_pair[:, span]
        q, s = code(total)
        w_tot[u, :, span] = total
        wq_out[:, span] = q
        ws_out[:, span] = s
    w_copies = []
    for j, d in enumerate(order):
        w_copies.append(remote(wq_out, wq_in.at[j], wq_sem.at[j], {"blk": target(d)}))
        w_copies.append(remote(ws_out, ws_in.at[j], ws_sem.at[j], {"blk": target(d)}))
    for copy in w_copies:
        copy.start()

    sent = []
    for j in range(len(order)):
        sent.append(send_piece(j))

    for copy in w_copies:
        copy.wait()
    for first in range(0, half, LANES):
        span = slice(first, first + LANES)
        total = w_tot[u, :, span]
        for j in range(len(order)):
            total += value_of(wq_in[j, :, span], ws_in[j, :, span])
        w_tot[u, :, span] = total
    t_copy = remote(w_tot.at[u], w_tot.at[u], wt_sem, {"yr": sib})
    t_copy.start()
    chunk = 256
    for first in range(0, units, chunk):
        lane_of = lax.broadcasted_iota(jnp.int32, (LANES, chunk), 0)
        hot = jnp.where(lane_of == (col_ref[:, first:first + chunk] & 127), 1.0, 0.0)
        onel[first:first + chunk, :] = jnp.transpose(hot).astype(jnp.bfloat16)
    t_copy.wait()
    for h in range(2):
        total = w_tot[h]
        hi = total.astype(jnp.bfloat16)
        w_hl[:rows, h * half:(h + 1) * half] = hi
        w_hl[rows:, h * half:(h + 1) * half] = (total - hi.astype(jnp.float32)).astype(jnp.bfloat16)
    mine = (2 * b + u) * per

    def place(i, carry):
        mask = jnp.where((col_ref[...] >> 7) == mine + i, 1.0, 0.0).astype(jnp.bfloat16)
        both = jnp.dot(w_hl[...] * mask, onel[...], preferred_element_type=jnp.float32)
        placed[i] = both[:rows] + both[rows:]
        return carry

    lax.fori_loop(0, per, place, 0)

    pair_copies[-1].wait()
    for copies in sent:
        for copy in copies:
            copy.wait()

    def finish(i, carry):
        total = acc_ref[mine + i] + pair[nb - 1, i] + placed[i]
        for j in range(len(order)):
            total += value_of(q_in[j, i], s_in[j, pl.ds(i, 1)])
        out_ref[:, pl.ds(pl.multiple_of(i * LANES, LANES), LANES)] = total
        return carry

    lax.fori_loop(0, per, finish, 0)

    for copy in small:
        copy.wait()
    dots = d_ref[...]
    for dc in range(1, nc):
        dots += d_in[dc - 1]
    for dc in range(nc):
        dots += e_in[dc]
    intercept_ref[...] = objective_ref[...] - jnp.transpose(dots)[:objective_ref.shape[0], :]


def local(nb, nc, price, avail, tile_ids, soc, link, retain, store_col, weight, capacity, objective):
    years, weeks, tiles, hours, width = avail.shape
    rows, units = soc.shape[2:]
    columns = capacity.shape[0]
    tile_count = columns // width
    steps = years * weeks
    piece = columns // (2 * nb)
    per = piece // width
    half = units // 2
    retain2 = retain.reshape(1, units)
    col2 = store_col.reshape(1, units)
    f32 = jnp.float32

    def week(g, *_):
        return (g // weeks, lax.rem(g, weeks), 0, 0)

    def fixed(rank):
        return lambda g, *_: (0,) * rank

    acc, wsum, d, e = pl.pallas_call(
        functools.partial(local_kernel, years, weeks),
        grid_spec=pltpu.PrefetchScalarGridSpec(
            num_scalar_prefetch=2,
            grid=(steps,),
            in_specs=[
                pl.BlockSpec((1, 1, rows, hours), week),
                pl.BlockSpec((1, 1, tiles, hours, width), lambda g, *_: (g // weeks, lax.rem(g, weeks), 0, 0, 0)),
                pl.BlockSpec((1, 1, rows, units), week),
                pl.BlockSpec((1, 1, rows, units), week),
                pl.BlockSpec((1, units), fixed(2)),
                pl.BlockSpec((1, units), fixed(2)),
                pl.BlockSpec((tile_count, 1, width), fixed(3)),
            ],
            out_specs=[
                pl.BlockSpec((tile_count, rows, width), fixed(3)),
                pl.BlockSpec((rows, units), fixed(2)),
                pl.BlockSpec((rows, LANES), fixed(2)),
                pl.BlockSpec((rows, LANES), fixed(2)),
            ],
            scratch_shapes=[pltpu.VMEM((1, units), f32)],
        ),
        out_shape=[
            jax.ShapeDtypeStruct((tile_count, rows, width), f32),
            jax.ShapeDtypeStruct((rows, units), f32),
            jax.ShapeDtypeStruct((rows, LANES), f32),
            jax.ShapeDtypeStruct((rows, LANES), f32),
        ],
        compiler_params=pltpu.CompilerParams(vmem_limit_bytes=60 * 1024 * 1024),
    )(tile_ids, weight, price, avail, soc, link, retain2, col2, capacity.reshape(tile_count, 1, width))

    tail = jnp.broadcast_to(weight[:, weeks - 1][:, None, None], (years, 1, LANES))
    vmem = pl.BlockSpec(memory_space=pltpu.VMEM)
    dma = pltpu.SemaphoreType.DMA
    out, intercept = pl.pallas_call(
        functools.partial(reduce_kernel, nb, nc),
        grid=(1,),
        in_specs=[vmem, vmem, pl.BlockSpec((years, 1, rows, units), lambda g: (0, 0, 0, 0))] + [vmem] * 6,
        out_specs=[vmem, vmem],
        out_shape=[
            jax.ShapeDtypeStruct((rows, piece), f32),
            jax.ShapeDtypeStruct((steps, rows), f32),
        ],
        scratch_shapes=[
            pltpu.VMEM((nb, per, rows, width), f32),
            pltpu.VMEM((nb - 1, per, rows, width), jnp.int16),
            pltpu.VMEM((nb - 1, per, width), f32),
            pltpu.VMEM((nb - 1, per, rows, width), jnp.int16),
            pltpu.VMEM((nb - 1, per, width), f32),
            pltpu.VMEM((years, 1, LANES), f32),
            pltpu.VMEM((max(nc - 1, 1), rows, LANES), f32),
            pltpu.VMEM((nc, rows, LANES), f32),
            pltpu.VMEM((2, rows, half), f32),
            pltpu.VMEM((rows, half), f32),
            pltpu.VMEM((rows, half), jnp.int16),
            pltpu.VMEM((1, half), f32),
            pltpu.VMEM((nb - 1, rows, half), jnp.int16),
            pltpu.VMEM((nb - 1, 1, half), f32),
            pltpu.VMEM((2, rows, half), f32),
            pltpu.VMEM((2 * rows, units), jnp.bfloat16),
            pltpu.VMEM((units, LANES), jnp.bfloat16),
            pltpu.VMEM((per, rows, width), f32),
            dma((nb, 2)),
            dma((nb - 1, 2)),
            dma((nb - 1, 2)),
            dma((2,)),
            dma((max(nc - 1, 1), 2)),
            dma((nc, 2)),
            dma((2,)),
            dma((nb - 1, 2)),
            dma((nb - 1, 2)),
            dma((2,)),
        ],
        compiler_params=pltpu.CompilerParams(
            collective_id=0, has_side_effects=True, vmem_limit_bytes=VMEM_LIMIT
        ),
    )(acc, wsum, link, retain2, tail, d, e, col2, objective.reshape(steps, rows))
    return (out[:, None, :], intercept.reshape(years, weeks, rows))


def solution(mesh):
    return jax.shard_map(
        functools.partial(local, mesh.shape["blk"], mesh.shape["cap"]),
        mesh=mesh,
        in_specs=(
            P(("groups", "yr"), "blk", None, None),
            P(("groups", "yr"), "blk", "cap", None, None),
            P(("groups", "yr"), "blk", "cap"),
            P(("groups", "yr"), "blk", None, "cap"),
            P(("groups", "yr"), "blk", None, "cap"),
            P("cap"),
            P("cap"),
            P(("groups", "yr"), "blk"),
            P("cap"),
            P(("groups", "yr"), "blk", None),
        ),
        out_specs=(P("groups", "cap", ("blk", "yr")), P(("groups", "yr"), "blk", None)),
        check_vma=False,
    )
```
